32 devices in a mesh: region: 2 (over x), sub: 16 (over z, y, core).
Axes of the slice: x: 2, y: 2, z: 4, core: 2. Of those that a mesh axis runs over, the one named last changes fastest.
Arguments:
- right_side: bfloat16 [2, 16, 1024, 256], P('region', 'sub'), may hold values from -6 to 6
- local_inverse: bfloat16 [2, 16, 1024, 1024], P('region', 'sub')
- coupling: bfloat16 [2, 16, 4, 256, 256], P('region', 'sub'), may hold values from -0.75 to 0.75
- margin_blocks: int32 [4, 2, 16, 2], P(None, 'region', 'sub'), may hold values from 0 to 7, as said below
- partner: int32 [4, 32], replicated, may hold values from 0 to 31, as said below
- restriction: bfloat16 [2, 16, 64, 1024], P('region', 'sub'), may hold values from -0.375 to 0.375
- coarse_rows: bfloat16 [2, 1024, 1024], P('region', 'sub')
Outputs:
- solution: bfloat16 [2, 16, 1024, 256], P('region', 'sub')
The draws below stay inside these ranges and needn't reach their ends.
Inputs may be any that keep to these rules, and one draw needn't show every extreme that they name: `margin_blocks`: for each colour, subdomain and k, a block number below 8; the 2 numbers of one colour and subdomain are distinct. For each colour a perfect matching of all subdomains: the partner of a subdomain's partner is the subdomain itself, and no subdomain is its own partner.
All inputs are finite; a program needn't handle non-finite values.
Results may differ from the reference program's by a relative error of at most 0.0052.
Values may be sent and summed in bfloat16 or wider, within the bound.
A program may use at most 64 MiB of HBM per device.

```python
import jax
import jax.numpy as jnp
from jax import lax

SUB_ROWS = 1024
NRHS = 256
BLK = 128
OVL_BLK = 2
COLORS = 4
CP = 64
REGIONS = 2
SUBS = 16
OVL = 256


def dominant_square(key, leading, order, scale_low, scale_high):

    def one_slab(index):
        slab_key = jax.random.fold_in(key, index)
        first_key, second_key = jax.random.split(slab_key)
        scatter_part = jax.random.normal(first_key, leading[1:] + (order, order), jnp.float32) * (0.7 / jnp.sqrt(jnp.float32(order)))
        diagonal_part = jax.random.uniform(second_key, leading[1:] + (order,), jnp.float32, scale_low, scale_high)
        return scatter_part + jnp.eye(order, dtype=jnp.float32) * diagonal_part[..., None, :]
    return lax.map(one_slab, jnp.arange(leading[0], dtype=jnp.int32))


def draw_local_inverse(key, part):
    return dominant_square(jax.random.fold_in(key, 11), (REGIONS, SUBS), SUB_ROWS, 1.0, 2.0).astype(jnp.bfloat16)


def draw_coarse_rows(key, part):
    return dominant_square(jax.random.fold_in(key, 23), (REGIONS,), SUBS * CP, 1.0, 2.0).astype(jnp.bfloat16)


def draw_margin_blocks(key, part):
    block_count = SUB_ROWS // BLK
    scores = jax.random.randint(jax.random.fold_in(key, 37), (COLORS, REGIONS, SUBS, block_count), 0, 1 << 20)
    scores = scores * block_count + jnp.arange(block_count, dtype=jnp.int32)
    ordered = jnp.argsort(scores, axis=-1, stable=True).astype(jnp.int32)
    return ordered[..., :OVL_BLK]


def matching(key, members):
    shuffled = jax.random.permutation(key, members).astype(jnp.int32)
    paired = shuffled.reshape(members // 2, 2)
    mates = jnp.zeros((members,), jnp.int32)
    mates = mates.at[paired[:, 0]].set(paired[:, 1])
    return mates.at[paired[:, 1]].set(paired[:, 0])


def draw_partner(key, part):
    colour_keys = jax.random.split(jax.random.fold_in(key, 41), COLORS)
    return jax.vmap(lambda single: matching(single, REGIONS * SUBS))(colour_keys)


def steps_of(rng, dims, cuts, smallest, largest):
    factor_of = 1.0
    for axis_at, parts in cuts:
        steps = jax.random.uniform(jax.random.fold_in(jax.random.fold_in(rng, 6), axis_at), (parts,), jnp.float32, smallest / len(cuts), largest / len(cuts))
        factor_of = factor_of * jnp.repeat(jnp.exp(steps), dims[axis_at] // parts).reshape((-1,) + (1,) * (len(dims) - 1 - axis_at))
    return factor_of


def noise(own_key, dims, scale, limit, pieces=(), held_as=jnp.bfloat16):
    result = scale * jax.random.normal(own_key, dims, jnp.float32)
    if pieces:
        result = result * steps_of(own_key, dims, pieces, -0.22, 0.18)
    return jnp.clip(result, -limit, limit).astype(held_as)


def setup_inputs(seed: int = 0) -> dict:
    key_list = jax.random.split(jax.random.key(seed), 8)
    right_side = noise(key_list[0], (REGIONS, SUBS, SUB_ROWS, NRHS), 1.0, 6.0, ((0, 2), (1, 16)))
    local_inverse = draw_local_inverse(jax.random.fold_in(key_list[7], 71), 0)
    coupling = noise(key_list[2], (REGIONS, SUBS, COLORS, OVL, OVL), (OVL // 4) ** -0.5, 0.75, ((0, 2), (1, 16)))
    margin_blocks = draw_margin_blocks(jax.random.fold_in(key_list[7], 71), 0)
    partner = draw_partner(jax.random.fold_in(key_list[7], 71), 0)
    restriction = noise(key_list[5], (REGIONS, SUBS, CP, SUB_ROWS), (SUB_ROWS // 4) ** -0.5, 0.375, ((0, 2), (1, 16)))
    coarse_rows = draw_coarse_rows(jax.random.fold_in(key_list[7], 71), 0)
    return dict(right_side=right_side, local_inverse=local_inverse, coupling=coupling, margin_blocks=margin_blocks, partner=partner, restriction=restriction, coarse_rows=coarse_rows)


def region_product(inputs_pair):
    return jnp.einsum("sab,sbn->san", inputs_pair[0].astype(jnp.float32), inputs_pair[1].astype(jnp.float32))


def coarse_product(inputs_pair):
    return jnp.dot(inputs_pair[0].astype(jnp.float32), inputs_pair[1].astype(jnp.float32)).astype(jnp.bfloat16)


def reference(right_side, local_inverse, coupling, margin_blocks, partner, restriction, coarse_rows):
    block_count = SUB_ROWS // BLK
    residual = right_side.astype(jnp.float32)
    accumulated = jnp.zeros(residual.shape, jnp.float32)
    for colour in range(COLORS):
        picked = margin_blocks[colour]
        tiled = residual.reshape(REGIONS, SUBS, block_count, BLK, NRHS)
        sent_rows = jnp.take_along_axis(tiled, picked[:, :, :, None, None], axis=2)
        sent_rows = sent_rows.reshape(REGIONS * SUBS, OVL, NRHS).astype(jnp.bfloat16)
        received = jnp.take(sent_rows, partner[colour], axis=0).reshape(REGIONS, SUBS, OVL, NRHS)
        coupled = jnp.einsum("gsab,gsbn->gsan", coupling[:, :, colour].astype(jnp.float32), received.astype(jnp.float32))
        one_hot = (picked[..., None] == jnp.arange(block_count, dtype=jnp.int32)).astype(jnp.float32)
        added = jnp.einsum("gskb,gskin->gsbin", one_hot, coupled.reshape(REGIONS, SUBS, OVL_BLK, BLK, NRHS))
        widened = residual + added.reshape(REGIONS, SUBS, SUB_ROWS, NRHS)
        shaped = widened.astype(jnp.bfloat16)
        correction = lax.map(region_product, (local_inverse, shaped))
        accumulated = accumulated + correction
        residual = widened - 0.25 * correction
    settled = residual.astype(jnp.bfloat16)
    projected = jnp.einsum("gscr,gsrn->gscn", restriction.astype(jnp.float32), settled.astype(jnp.float32)).astype(jnp.bfloat16)
    stacked = projected.reshape(REGIONS, SUBS * CP, NRHS)
    coarse = lax.map(coarse_product, (coarse_rows, stacked)).reshape(REGIONS, SUBS, CP, NRHS)
    lifted = jnp.einsum("gscr,gscn->gsrn", restriction.astype(jnp.float32), coarse.astype(jnp.float32))
    return (accumulated + lifted).astype(jnp.bfloat16)
```

```python
import functools

import jax
import jax.numpy as jnp
from jax import lax
from jax.experimental import pallas as pl
from jax.experimental.pallas import tpu as pltpu
from jax.sharding import PartitionSpec as P

BLK = 128
OVL_BLK = 2
COLORS = 4
TILE_ROWS = 16
TILE_COLS = 128
MESH = pl.DeviceIdType.MESH


def sweep(
    regions,
    subs,
    right_ref,
    inverse_ref,
    coupling_ref,
    blocks_ref,
    partner_ref,
    restriction_ref,
    coarse_ref,
    out_ref,
    residual,
    accumulated,
    shaped,
    outgoing,
    arrived,
    forwarded,
    received,
    stacked,
    sem_spread_out,
    sem_spread_in,
    sem_back_out,
    sem_back_in,
    sem_gather_out,
    sem_gather_in,
    sem_pair_out,
    sem_pair_in,
):
    count = regions * subs
    region, sub = lax.axis_index("region"), lax.axis_index("sub")
    me = region * subs + sub
    block_count, _, columns = right_ref.shape
    rows = block_count * BLK
    span = OVL_BLK * BLK
    row_tiles, col_tiles = span // TILE_ROWS, columns // TILE_COLS
    pieces = row_tiles * col_tiles
    stride = count // pieces
    slot = me // stride
    is_relay = lax.rem(me, stride) == 0
    cp = restriction_ref.shape[0]

    def place(number):
        return (number // subs, lax.rem(number, subs))

    barrier = pltpu.get_barrier_semaphore()

    def greet(step, carry):
        other = lax.rem(me + step, count)
        pl.semaphore_signal(barrier, inc=1, device_id=place(other), device_id_type=MESH)
        return carry

    lax.fori_loop(1, count, greet, 0)

    def spread_copy(colour, piece):
        return pltpu.make_async_remote_copy(
            src_ref=outgoing.at[colour, piece],
            dst_ref=arrived[colour].at[me],
            send_sem=sem_spread_out.at[colour],
            recv_sem=sem_spread_in.at[colour],
            device_id=place(piece * stride),
            device_id_type=MESH,
        )

    def back_copy(colour, owner):
        return pltpu.make_async_remote_copy(
            src_ref=forwarded.at[colour, owner],
            dst_ref=received.at[colour, slot],
            send_sem=sem_back_out.at[colour],
            recv_sem=sem_back_in.at[colour],
            device_id=place(owner),
            device_id_type=MESH,
        )

    def wait_bytes(buffer, number, sem):
        view = buffer.at[pl.ds(0, number)]
        pltpu.make_async_copy(view, view, sem).wait()

    def on_relay(body):
        if stride == 1:
            body()
        else:
            pl.when(is_relay)(body)

    def off_relay(body):
        if stride > 1:
            pl.when(jnp.logical_not(is_relay))(body)

    def spread(colour, k, values):
        half = BLK // TILE_ROWS
        for col in range(col_tiles):
            block = values[:, col * TILE_COLS : (col + 1) * TILE_COLS]
            first = col * row_tiles + k * half
            outgoing[colour, first : first + half] = block.reshape(half, TILE_ROWS, TILE_COLS)

    def start_spread(colour):
        def send(step, carry):
            spread_copy(colour, lax.rem(slot + step, pieces)).start()
            return carry

        lax.fori_loop(1, pieces, send, 0)

        @on_relay
        def _():
            arrived[colour][me] = outgoing[colour, slot]

        @off_relay
        def _():
            spread_copy(colour, slot).start()

    def relay(colour):
        @on_relay
        def _():
            wait_bytes(arrived[colour], count - 1, sem_spread_in.at[colour])

            def send(step, carry):
                owner = lax.rem(me + step, count)
                forwarded[colour, owner] = arrived[colour][partner_ref[colour, owner]]
                back_copy(colour, owner).start()
                return carry

            lax.fori_loop(1, count, send, 0)
            received[colour, slot] = arrived[colour][partner_ref[colour, me]]

    def collect(colour):
        @on_relay
        def _():
            wait_bytes(received.at[colour], pieces - 1, sem_back_in.at[colour])

        @off_relay
        def _():
            wait_bytes(received.at[colour], pieces, sem_back_in.at[colour])

    for k in range(OVL_BLK):
        spread(0, k, right_ref[blocks_ref[0, k]])
    pl.semaphore_wait(barrier, count - 1)
    start_spread(0)
    residual[...] = right_ref[...].astype(jnp.float32)

    for colour in range(COLORS):
        relay(colour)
        collect(colour)
        got = received[colour]
        got = jnp.concatenate(
            [
                got[c * row_tiles : (c + 1) * row_tiles].reshape(span, TILE_COLS)
                for c in range(col_tiles)
            ],
            axis=1,
        )
        coupled = jnp.dot(coupling_ref[colour], got, preferred_element_type=jnp.float32)
        for b in range(block_count):
            wide = residual[b]
            for k in range(OVL_BLK):
                apart = blocks_ref[colour, k] - b
                chosen = (1 - jnp.minimum(apart * apart, 1)).astype(jnp.float32)
                wide = wide + chosen * coupled[k * BLK : (k + 1) * BLK]
            residual[b] = wide
            shaped[b * BLK : (b + 1) * BLK, :] = wide.astype(jnp.bfloat16)
        if colour + 1 < COLORS:
            for k in range(OVL_BLK):
                block = blocks_ref[colour + 1, k]
                fix = jnp.dot(
                    inverse_ref[block], shaped[...], preferred_element_type=jnp.float32
                )
                left = residual[block] - 0.25 * fix
                spread(colour + 1, k, left.astype(jnp.bfloat16))
            start_spread(colour + 1)
        for b in range(0, block_count, 2):
            fix = jnp.dot(
                inverse_ref[b : b + 2].reshape(2 * BLK, rows),
                shaped[...],
                preferred_element_type=jnp.float32,
            ).reshape(2, BLK, columns)
            if colour == 0:
                accumulated[b : b + 2] = fix
            else:
                accumulated[b : b + 2] = accumulated[b : b + 2] + fix
            residual[b : b + 2] = residual[b : b + 2] - 0.25 * fix

    projected = jnp.dot(
        restriction_ref[...],
        residual[...].astype(jnp.bfloat16).reshape(rows, columns),
        preferred_element_type=jnp.float32,
    )
    stacked[sub] = projected.astype(jnp.bfloat16)

    chips = subs // 2
    core = lax.rem(sub, 2)
    mate = sub + 1 - 2 * core

    def gather_copy(step):
        return pltpu.make_async_remote_copy(
            src_ref=stacked.at[sub],
            dst_ref=stacked.at[sub],
            send_sem=sem_gather_out.at[step],
            recv_sem=sem_gather_in.at[step],
            device_id=(region, lax.rem(sub + 2 * step, subs)),
            device_id_type=MESH,
        )

    def pair_copy(step):
        from_sub = lax.rem(sub + subs - 2 * step, subs)
        return pltpu.make_async_remote_copy(
            src_ref=stacked.at[from_sub],
            dst_ref=stacked.at[from_sub],
            send_sem=sem_pair_out.at[step],
            recv_sem=sem_pair_in.at[step],
            device_id=(region, mate),
            device_id_type=MESH,
        )

    for step in range(1, chips):
        gather_copy(step).start()
    pair_copy(0).start()
    for step in range(1, chips):
        gather_copy(step).wait_recv()
        pair_copy(step).start()
    for step in range(chips):
        pair_copy(step).wait_recv()
    everything = stacked[...].reshape(subs * cp, columns)
    coarse = jnp.dot(coarse_ref[...], everything, preferred_element_type=jnp.float32)
    coarse = coarse.astype(jnp.bfloat16)
    lifted = lax.dot_general(
        restriction_ref[...], coarse, (((0,), (0,)), ((), ())), preferred_element_type=jnp.float32
    )
    lifted = lifted.reshape(block_count, BLK, columns)
    out_ref[...] = (accumulated[...] + lifted).astype(jnp.bfloat16)

    for step in range(1, chips):
        gather_copy(step).wait_send()
    for step in range(chips):
        pair_copy(step).wait_send()
    for colour in range(COLORS):

        @on_relay
        def _():
            wait_bytes(outgoing.at[colour], pieces - 1, sem_spread_out.at[colour])
            wait_bytes(forwarded.at[colour], count - 1, sem_back_out.at[colour])

        @off_relay
        def _():
            wait_bytes(outgoing.at[colour], pieces, sem_spread_out.at[colour])


def shards(right_side, local_inverse, coupling, margin_blocks, partner, restriction, coarse_rows):
    regions, subs = lax.axis_size("region"), lax.axis_size("sub")
    count = regions * subs
    right = right_side[0, 0]
    rows, columns = right.shape
    pieces = OVL_BLK * BLK * columns // (TILE_ROWS * TILE_COLS)
    cp = restriction.shape[2]
    piece = (TILE_ROWS, TILE_COLS)
    blocked = (rows // BLK, BLK, columns)
    vmem = pl.BlockSpec(memory_space=pltpu.VMEM)
    smem = pl.BlockSpec(memory_space=pltpu.SMEM)
    dma = pltpu.SemaphoreType.DMA
    result = pl.pallas_call(
        functools.partial(sweep, regions, subs),
        out_shape=jax.ShapeDtypeStruct(blocked, jnp.bfloat16),
        in_specs=[vmem, vmem, vmem, smem, smem, vmem, vmem],
        out_specs=vmem,
        scratch_shapes=[
            pltpu.VMEM(blocked, jnp.float32),
            pltpu.VMEM(blocked, jnp.float32),
            pltpu.VMEM((rows, columns), jnp.bfloat16),
            pltpu.VMEM((COLORS, pieces) + piece, jnp.bfloat16),
            [pltpu.VMEM((count,) + piece, jnp.bfloat16) for _ in range(COLORS)],
            pltpu.VMEM((COLORS, count) + piece, jnp.bfloat16),
            pltpu.VMEM((COLORS, pieces) + piece, jnp.bfloat16),
            pltpu.VMEM((subs, cp, columns), jnp.bfloat16),
            dma((COLORS,)),
            dma((COLORS,)),
            dma((COLORS,)),
            dma((COLORS,)),
            dma((subs // 2,)),
            dma((subs // 2,)),
            dma((subs // 2,)),
            dma((subs // 2,)),
        ],
        compiler_params=pltpu.CompilerParams(
            collective_id=0, has_side_effects=True, vmem_limit_bytes=48 * 1024 * 1024
        ),
    )(
        right.reshape(blocked),
        local_inverse.reshape(rows // BLK, BLK, rows),
        coupling[0, 0],
        margin_blocks[:, 0, 0, :],
        partner,
        restriction[0, 0],
        coarse_rows[0],
    )
    return result.reshape(right_side.shape)


def solution(mesh):
    placed = (
        P("region", "sub", None, None),
        P("region", "sub", None, None),
        P("region", "sub", None, None, None),
        P(None, "region", "sub", None),
        P(),
        P("region", "sub", None, None),
        P("region", "sub", None),
    )
    return jax.shard_map(
        shards,
        mesh=mesh,
        in_specs=placed,
        out_specs=P("region", "sub", None, None),
        check_vma=False,
    )
```

```python
import functools

import jax
import jax.numpy as jnp
from jax import lax
from jax.experimental import pallas as pl
from jax.experimental.pallas import tpu as pltpu
from jax.sharding import PartitionSpec as P

BLK = 128
OVL_BLK = 2
COLORS = 4
TILE_ROWS = 16
TILE_COLS = 128
UNROLL = False
MESH = pl.DeviceIdType.MESH


def sweep(
    regions,
    subs,
    right_hbm,
    inverse_hbm,
    coupling_hbm,
    blocks_ref,
    partner_ref,
    restriction_hbm,
    coarse_hbm,
    out_ref,
    right_ref,
    inverse_ref,
    coupling_ref,
    restriction_ref,
    coarse_ref,
    sem_load,
    residual,
    accumulated,
    shaped,
    outgoing,
    arrived,
    forwarded,
    received,
    stacked,
    sem_spread_out,
    sem_spread_in,
    sem_back_out,
    sem_back_in,
    sem_gather_out,
    sem_gather_in,
    sem_pair_out,
    sem_pair_in,
):
    count = regions * subs
    region, sub = lax.axis_index("region"), lax.axis_index("sub")
    me = region * subs + sub
    block_count, _, columns = right_hbm.shape
    rows = block_count * BLK
    span = OVL_BLK * BLK
    row_tiles, col_tiles = span // TILE_ROWS, columns // TILE_COLS
    pieces = row_tiles * col_tiles
    stride = count // pieces
    slot = me // stride
    my_half, my_tile = lax.rem(slot, col_tiles), slot // col_tiles
    my_piece = my_half * row_tiles + my_tile
    is_relay = lax.rem(me, stride) == 0
    cp = restriction_hbm.shape[0]

    def place(number):
        return (number // subs, lax.rem(number, subs))

    loads = [
        pltpu.make_async_copy(source, target, sem_load.at[i])
        for i, (source, target) in enumerate(
            [
                (right_hbm, right_ref),
                (coupling_hbm, coupling_ref),
                (inverse_hbm, inverse_ref),
                (restriction_hbm, restriction_ref),
                (coarse_hbm, coarse_ref),
            ]
        )
    ]
    for load in loads:
        load.start()

    barrier = pltpu.get_barrier_semaphore()

    def greet(step, carry):
        other = lax.rem(me + step, count)
        pl.semaphore_signal(barrier, inc=1, device_id=place(other), device_id_type=MESH)
        return carry

    lax.fori_loop(1, count, greet, 0)

    def spread_copy(colour, half, tile):
        piece = half * row_tiles + tile
        return pltpu.make_async_remote_copy(
            src_ref=outgoing.at[colour, piece],
            dst_ref=arrived[colour].at[me],
            send_sem=sem_spread_out.at[colour],
            recv_sem=sem_spread_in.at[colour],
            device_id=place((tile * col_tiles + half) * stride),
            device_id_type=MESH,
        )

    def back_copy(colour, owner):
        return pltpu.make_async_remote_copy(
            src_ref=forwarded.at[colour, owner],
            dst_ref=received.at[colour, my_piece],
            send_sem=sem_back_out.at[colour],
            recv_sem=sem_back_in.at[colour, my_half],
            device_id=place(owner),
            device_id_type=MESH,
        )

    def wait_bytes(buffer, number, sem):
        view = buffer.at[pl.ds(0, number)]
        pltpu.make_async_copy(view, view, sem).wait()

    def on_relay(body):
        if stride == 1:
            body()
        else:
            pl.when(is_relay)(body)

    def off_relay(body):
        if stride > 1:
            pl.when(jnp.logical_not(is_relay))(body)

    def own_half(half):
        if stride == 1:
            return my_half == half
        return jnp.logical_and(is_relay, my_half == half)

    def lanes(half):
        return slice(half * TILE_COLS, (half + 1) * TILE_COLS)

    def spread(colour, half, k, values):
        tiles = BLK // TILE_ROWS
        first = half * row_tiles + k * tiles
        outgoing[colour, first : first + tiles] = values.reshape(tiles, TILE_ROWS, TILE_COLS)

    def start_spread(colour, half):
        def send(step, carry):
            spread_copy(colour, half, lax.rem(my_tile + step, row_tiles)).start()
            return carry

        lax.fori_loop(1, row_tiles, send, 0, unroll=UNROLL)

        @pl.when(own_half(half))
        def _():
            arrived[colour][me] = outgoing[colour, my_piece]

        @pl.when(jnp.logical_not(own_half(half)))
        def _():
            spread_copy(colour, half, my_tile).start()

    def relay(colour):
        @on_relay
        def _():
            wait_bytes(arrived[colour], count - 1, sem_spread_in.at[colour])

            def send(step, carry):
                owner = lax.rem(me + step, count)
                forwarded[colour, owner] = arrived[colour][partner_ref[colour, owner]]
                back_copy(colour, owner).start()
                return carry

            lax.fori_loop(1, count, send, 0, unroll=UNROLL)
            received[colour, my_piece] = arrived[colour][partner_ref[colour, me]]

    def collect(colour, half):
        @pl.when(own_half(half))
        def _():
            wait_bytes(received.at[colour], row_tiles - 1, sem_back_in.at[colour, half])

        @pl.when(jnp.logical_not(own_half(half)))
        def _():
            wait_bytes(received.at[colour], row_tiles, sem_back_in.at[colour, half])

    def correct(colour, half):
        part = lanes(half)
        for b in range(0, block_count, 2):
            fix = jnp.dot(
                inverse_ref[b : b + 2].reshape(2 * BLK, rows),
                shaped[:, part],
                preferred_element_type=jnp.float32,
            ).reshape(2, BLK, TILE_COLS)
            if colour == 0:
                accumulated[b : b + 2, :, part] = fix
            else:
                accumulated[b : b + 2, :, part] = accumulated[b : b + 2, :, part] + fix
            residual[b : b + 2, :, part] = residual[b : b + 2, :, part] - 0.25 * fix

    chips = subs // 2
    core = lax.rem(sub, 2)
    mate = sub + 1 - 2 * core

    def gather_copy(half, step):
        return pltpu.make_async_remote_copy(
            src_ref=stacked.at[half, sub],
            dst_ref=stacked.at[half, sub],
            send_sem=sem_gather_out.at[half, step],
            recv_sem=sem_gather_in.at[half, step],
            device_id=(region, lax.rem(sub + 2 * step, subs)),
            device_id_type=MESH,
        )

    def pair_copy(half, step):
        from_sub = lax.rem(sub + subs - 2 * step, subs)
        return pltpu.make_async_remote_copy(
            src_ref=stacked.at[half, from_sub],
            dst_ref=stacked.at[half, from_sub],
            send_sem=sem_pair_out.at[half, step],
            recv_sem=sem_pair_in.at[half, step],
            device_id=(region, mate),
            device_id_type=MESH,
        )

    halves = range(col_tiles)
    loads[0].wait()
    for half in halves:
        for k in range(OVL_BLK):
            spread(0, half, k, right_ref[blocks_ref[k, 0]][:, lanes(half)])
    pl.semaphore_wait(barrier, count - 1)
    for half in halves:
        start_spread(0, half)
    residual[...] = right_ref[...].astype(jnp.float32)
    for load in loads[1:]:
        load.wait()

    for colour in range(COLORS):
        relay(colour)
        for half in halves:
            part = lanes(half)
            collect(colour, half)
            got = received[colour, half * row_tiles : (half + 1) * row_tiles]
            coupled = jnp.dot(
                coupling_ref[colour],
                got.reshape(span, TILE_COLS),
                preferred_element_type=jnp.float32,
            )
            for b in range(block_count):
                wide = residual[b, :, part]
                for k in range(OVL_BLK):
                    apart = blocks_ref[k, colour] - b
                    chosen = (1 - jnp.minimum(apart * apart, 1)).astype(jnp.float32)
                    wide = wide + chosen * coupled[k * BLK : (k + 1) * BLK]
                residual[b, :, part] = wide
                shaped[b * BLK : (b + 1) * BLK, part] = wide.astype(jnp.bfloat16)
            if colour + 1 < COLORS:
                for k in range(OVL_BLK):
                    block = blocks_ref[k, colour + 1]
                    fix = jnp.dot(
                        inverse_ref[block], shaped[:, part], preferred_element_type=jnp.float32
                    )
                    left = residual[block][:, part] - 0.25 * fix
                    spread(colour + 1, half, k, left.astype(jnp.bfloat16))
                start_spread(colour + 1, half)
            else:
                correct(colour, half)
                projected = jnp.dot(
                    restriction_ref[...],
                    residual[:, :, part].astype(jnp.bfloat16).reshape(rows, TILE_COLS),
                    preferred_element_type=jnp.float32,
                )
                stacked[half, sub] = projected.astype(jnp.bfloat16)
                for step in range(1, chips):
                    gather_copy(half, step).start()
                pair_copy(half, 0).start()
        if colour + 1 < COLORS:
            for half in halves:
                correct(colour, half)

    for half in halves:
        for step in range(1, chips):
            gather_copy(half, step).wait_recv()
            pair_copy(half, step).start()
    for half in halves:
        part = lanes(half)
        for step in range(chips):
            pair_copy(half, step).wait_recv()
        coarse = jnp.dot(
            coarse_ref[...],
            stacked[half].reshape(subs * cp, TILE_COLS),
            preferred_element_type=jnp.float32,
        ).astype(jnp.bfloat16)
        lifted = lax.dot_general(
            restriction_ref[...],
            coarse,
            (((0,), (0,)), ((), ())),
            preferred_element_type=jnp.float32,
        ).reshape(block_count, BLK, TILE_COLS)
        out_ref[:, :, part] = (accumulated[:, :, part] + lifted).astype(jnp.bfloat16)

    for half in halves:
        for step in range(1, chips):
            gather_copy(half, step).wait_send()
        for step in range(chips):
            pair_copy(half, step).wait_send()
    for colour in range(COLORS):

        @on_relay
        def _():
            wait_bytes(outgoing.at[colour], pieces - 1, sem_spread_out.at[colour])
            wait_bytes(forwarded.at[colour], count - 1, sem_back_out.at[colour])

        @off_relay
        def _():
            wait_bytes(outgoing.at[colour], pieces, sem_spread_out.at[colour])


def shards(right_side, local_inverse, coupling, margin_blocks, partner, restriction, coarse_rows):
    regions, subs = lax.axis_size("region"), lax.axis_size("sub")
    count = regions * subs
    right = right_side[0, 0]
    rows, columns = right.shape
    pieces = OVL_BLK * BLK * columns // (TILE_ROWS * TILE_COLS)
    cp = restriction.shape[2]
    piece = (TILE_ROWS, TILE_COLS)
    blocked = (rows // BLK, BLK, columns)
    vmem = pl.BlockSpec(memory_space=pltpu.VMEM)
    smem = pl.BlockSpec(memory_space=pltpu.SMEM)
    hbm = pl.BlockSpec(memory_space=pltpu.HBM)
    bf16 = jnp.bfloat16
    halves = columns // TILE_COLS
    dma = pltpu.SemaphoreType.DMA
    result = pl.pallas_call(
        functools.partial(sweep, regions, subs),
        out_shape=jax.ShapeDtypeStruct(blocked, jnp.bfloat16),
        in_specs=[hbm, hbm, hbm, smem, smem, hbm, hbm],
        out_specs=vmem,
        scratch_shapes=[
            pltpu.VMEM(blocked, bf16),
            pltpu.VMEM((rows // BLK, BLK, rows), bf16),
            pltpu.VMEM(coupling.shape[2:], bf16),
            pltpu.VMEM(restriction.shape[2:], bf16),
            pltpu.VMEM(coarse_rows.shape[1:], bf16),
            dma((5,)),
            pltpu.VMEM(blocked, jnp.float32),
            pltpu.VMEM(blocked, jnp.float32),
            pltpu.VMEM((rows, columns), jnp.bfloat16),
            pltpu.VMEM((COLORS, pieces) + piece, jnp.bfloat16),
            [pltpu.VMEM((count,) + piece, jnp.bfloat16) for _ in range(COLORS)],
            pltpu.VMEM((COLORS, count) + piece, jnp.bfloat16),
            pltpu.VMEM((COLORS, pieces) + piece, jnp.bfloat16),
            pltpu.VMEM((halves, subs, cp, TILE_COLS), jnp.bfloat16),
            dma((COLORS,)),
            dma((COLORS,)),
            dma((COLORS,)),
            dma((COLORS, halves)),
            dma((halves, subs // 2)),
            dma((halves, subs // 2)),
            dma((halves, subs // 2)),
            dma((halves, subs // 2)),
        ],
        compiler_params=pltpu.CompilerParams(
            collective_id=0, has_side_effects=True, vmem_limit_bytes=56 * 1024 * 1024
        ),
    )(
        right.reshape(blocked),
        local_inverse.reshape(rows // BLK, BLK, rows),
        coupling[0, 0],
        margin_blocks[:, 0, 0, :].T,
        partner,
        restriction[0, 0],
        coarse_rows[0],
    )
    return result.reshape(right_side.shape)


def solution(mesh):
    placed = (
        P("region", "sub", None, None),
        P("region", "sub", None, None),
        P("region", "sub", None, None, None),
        P(None, "region", "sub", None),
        P(),
        P("region", "sub", None, None),
        P("region", "sub", None),
    )
    return jax.shard_map(
        shards,
        mesh=mesh,
        in_specs=placed,
        out_specs=P("region", "sub", None, None),
        check_vma=False,
    )
```

```python
import functools

import jax
import jax.numpy as jnp
from jax import lax
from jax.experimental import pallas as pl
from jax.experimental.pallas import tpu as pltpu
from jax.sharding import PartitionSpec as P

BLK = 128
OVL_BLK = 2
COLORS = 4
TILE_ROWS = 16
TILE_COLS = 128
UNROLL = False
MESH = pl.DeviceIdType.MESH


def sweep(
    regions,
    subs,
    right_hbm,
    inverse_hbm,
    coupling_hbm,
    blocks_hbm,
    partner_hbm,
    restriction_hbm,
    coarse_hbm,
    out_ref,
    blocks_ref,
    partner_ref,
    right_ref,
    inverse_ref,
    coupling_ref,
    restriction_ref,
    coarse_ref,
    sem_load,
    residual,
    accumulated,
    shaped,
    outgoing,
    arrived,
    forwarded,
    received,
    stacked,
    sem_spread_out,
    sem_spread_in,
    sem_back_out,
    sem_back_in,
    sem_gather_out,
    sem_gather_in,
    sem_pair_out,
    sem_pair_in,
):
    count = regions * subs
    region, sub = lax.axis_index("region"), lax.axis_index("sub")
    me = region * subs + sub
    block_count, _, columns = right_hbm.shape
    rows = block_count * BLK
    span = OVL_BLK * BLK
    row_tiles, col_tiles = span // TILE_ROWS, columns // TILE_COLS
    pieces = row_tiles * col_tiles
    stride = count // pieces
    slot = me // stride
    my_half, my_tile = lax.rem(slot, col_tiles), slot // col_tiles
    my_piece = my_half * row_tiles + my_tile
    is_relay = lax.rem(me, stride) == 0
    cp = restriction_hbm.shape[0]

    def place(number):
        return (number // subs, lax.rem(number, subs))

    loads = [
        pltpu.make_async_copy(source, target, sem_load.at[i])
        for i, (source, target) in enumerate(
            [
                (blocks_hbm, blocks_ref),
                (right_hbm, right_ref),
                (partner_hbm, partner_ref),
                (coupling_hbm, coupling_ref),
                (inverse_hbm, inverse_ref),
                (restriction_hbm, restriction_ref),
                (coarse_hbm, coarse_ref),
            ]
        )
    ]
    for load in loads:
        load.start()

    barrier = pltpu.get_barrier_semaphore()

    def greet(step, carry):
        other = lax.rem(me + step, count)
        pl.semaphore_signal(barrier, inc=1, device_id=place(other), device_id_type=MESH)
        return carry

    lax.fori_loop(1, count, greet, 0)

    def spread_copy(colour, half, tile):
        piece = half * row_tiles + tile
        return pltpu.make_async_remote_copy(
            src_ref=outgoing.at[colour, piece],
            dst_ref=arrived[colour].at[me],
            send_sem=sem_spread_out.at[colour],
            recv_sem=sem_spread_in.at[colour],
            device_id=place((tile * col_tiles + half) * stride),
            device_id_type=MESH,
        )

    def back_copy(colour, owner):
        return pltpu.make_async_remote_copy(
            src_ref=forwarded.at[colour, owner],
            dst_ref=received.at[colour, my_piece],
            send_sem=sem_back_out.at[colour],
            recv_sem=sem_back_in.at[colour, my_half],
            device_id=place(owner),
            device_id_type=MESH,
        )

    def wait_bytes(buffer, number, sem):
        view = buffer.at[pl.ds(0, number)]
        pltpu.make_async_copy(view, view, sem).wait()

    def on_relay(body):
        if stride == 1:
            body()
        else:
            pl.when(is_relay)(body)

    def off_relay(body):
        if stride > 1:
            pl.when(jnp.logical_not(is_relay))(body)

    def own_half(half):
        if stride == 1:
            return my_half == half
        return jnp.logical_and(is_relay, my_half == half)

    def lanes(half):
        return slice(half * TILE_COLS, (half + 1) * TILE_COLS)

    def spread(colour, half, k, values):
        tiles = BLK // TILE_ROWS
        first = half * row_tiles + k * tiles
        outgoing[colour, first : first + tiles] = values.reshape(tiles, TILE_ROWS, TILE_COLS)

    def start_spread(colour, half):
        def send(step, carry):
            spread_copy(colour, half, lax.rem(my_tile + step, row_tiles)).start()
            return carry

        lax.fori_loop(1, row_tiles, send, 0, unroll=UNROLL)

        @pl.when(own_half(half))
        def _():
            arrived[colour][me] = outgoing[colour, my_piece]

        @pl.when(jnp.logical_not(own_half(half)))
        def _():
            spread_copy(colour, half, my_tile).start()

    def relay(colour):
        @on_relay
        def _():
            wait_bytes(arrived[colour], count - 1, sem_spread_in.at[colour])

            def send(step, carry):
                owner = lax.rem(me + step, count)
                forwarded[colour, owner] = arrived[colour][partner_ref[colour, owner]]
                back_copy(colour, owner).start()
                return carry

            lax.fori_loop(1, count, send, 0, unroll=UNROLL)
            received[colour, my_piece] = arrived[colour][partner_ref[colour, me]]

    def collect(colour, half):
        @pl.when(own_half(half))
        def _():
            wait_bytes(received.at[colour], row_tiles - 1, sem_back_in.at[colour, half])

        @pl.when(jnp.logical_not(own_half(half)))
        def _():
            wait_bytes(received.at[colour], row_tiles, sem_back_in.at[colour, half])

    def correct(colour, half):
        part = lanes(half)
        for b in range(0, block_count, 2):
            fix = jnp.dot(
                inverse_ref[b : b + 2].reshape(2 * BLK, rows),
                shaped[:, part],
                preferred_element_type=jnp.float32,
            ).reshape(2, BLK, TILE_COLS)
            if colour == 0:
                accumulated[b : b + 2, :, part] = fix
            else:
                accumulated[b : b + 2, :, part] = accumulated[b : b + 2, :, part] + fix
            residual[b : b + 2, :, part] = residual[b : b + 2, :, part] - 0.25 * fix

    chips = subs // 2
    core = lax.rem(sub, 2)
    mate = sub + 1 - 2 * core

    def gather_copy(half, step):
        return pltpu.make_async_remote_copy(
            src_ref=stacked.at[half, sub],
            dst_ref=stacked.at[half, sub],
            send_sem=sem_gather_out.at[half, step],
            recv_sem=sem_gather_in.at[half, step],
            device_id=(region, lax.rem(sub + 2 * step, subs)),
            device_id_type=MESH,
        )

    def pair_copy(half, step):
        from_sub = lax.rem(sub + subs - 2 * step, subs)
        return pltpu.make_async_remote_copy(
            src_ref=stacked.at[half, from_sub],
            dst_ref=stacked.at[half, from_sub],
            send_sem=sem_pair_out.at[half, step],
            recv_sem=sem_pair_in.at[half, step],
            device_id=(region, mate),
            device_id_type=MESH,
        )

    halves = range(col_tiles)
    loads[0].wait()
    loads[1].wait()
    for half in halves:
        for k in range(OVL_BLK):
            spread(0, half, k, right_ref[blocks_ref[k, 0]][:, lanes(half)])
    pl.semaphore_wait(barrier, count - 1)
    for half in halves:
        start_spread(0, half)
    residual[...] = right_ref[...].astype(jnp.float32)
    for load in loads[2:]:
        load.wait()

    for colour in range(COLORS):
        relay(colour)
        for half in halves:
            part = lanes(half)
            collect(colour, half)
            got = received[colour, half * row_tiles : (half + 1) * row_tiles]
            coupled = jnp.dot(
                coupling_ref[colour],
                got.reshape(span, TILE_COLS),
                preferred_element_type=jnp.float32,
            )
            for b in range(block_count):
                wide = residual[b, :, part]
                for k in range(OVL_BLK):
                    apart = blocks_ref[k, colour] - b
                    chosen = (1 - jnp.minimum(apart * apart, 1)).astype(jnp.float32)
                    wide = wide + chosen * coupled[k * BLK : (k + 1) * BLK]
                residual[b, :, part] = wide
                shaped[b * BLK : (b + 1) * BLK, part] = wide.astype(jnp.bfloat16)
            if colour + 1 < COLORS:
                for k in range(OVL_BLK):
                    block = blocks_ref[k, colour + 1]
                    fix = jnp.dot(
                        inverse_ref[block], shaped[:, part], preferred_element_type=jnp.float32
                    )
                    left = residual[block][:, part] - 0.25 * fix
                    spread(colour + 1, half, k, left.astype(jnp.bfloat16))
                start_spread(colour + 1, half)
            else:
                correct(colour, half)
                projected = jnp.dot(
                    restriction_ref[...],
                    residual[:, :, part].astype(jnp.bfloat16).reshape(rows, TILE_COLS),
                    preferred_element_type=jnp.float32,
                )
                stacked[half, sub] = projected.astype(jnp.bfloat16)
                for step in range(1, chips):
                    gather_copy(half, step).start()
                pair_copy(half, 0).start()
        if colour + 1 < COLORS:
            for half in halves:
                correct(colour, half)

    for half in halves:
        for step in range(1, chips):
            gather_copy(half, step).wait_recv()
            pair_copy(half, step).start()
    for half in halves:
        part = lanes(half)
        for step in range(chips):
            pair_copy(half, step).wait_recv()
        coarse = jnp.dot(
            coarse_ref[...],
            stacked[half].reshape(subs * cp, TILE_COLS),
            preferred_element_type=jnp.float32,
        ).astype(jnp.bfloat16)
        lifted = lax.dot_general(
            restriction_ref[...],
            coarse,
            (((0,), (0,)), ((), ())),
            preferred_element_type=jnp.float32,
        ).reshape(block_count, BLK, TILE_COLS)
        out_ref[:, :, part] = (accumulated[:, :, part] + lifted).astype(jnp.bfloat16)

    for half in halves:
        for step in range(1, chips):
            gather_copy(half, step).wait_send()
        for step in range(chips):
            pair_copy(half, step).wait_send()
    for colour in range(COLORS):

        @on_relay
        def _():
            wait_bytes(outgoing.at[colour], pieces - 1, sem_spread_out.at[colour])
            wait_bytes(forwarded.at[colour], count - 1, sem_back_out.at[colour])

        @off_relay
        def _():
            wait_bytes(outgoing.at[colour], pieces, sem_spread_out.at[colour])


def shards(right_side, local_inverse, coupling, margin_blocks, partner, restriction, coarse_rows):
    regions, subs = lax.axis_size("region"), lax.axis_size("sub")
    count = regions * subs
    right = right_side[0, 0]
    rows, columns = right.shape
    pieces = OVL_BLK * BLK * columns // (TILE_ROWS * TILE_COLS)
    cp = restriction.shape[2]
    piece = (TILE_ROWS, TILE_COLS)
    blocked = (rows // BLK, BLK, columns)
    vmem = pl.BlockSpec(memory_space=pltpu.VMEM)
    hbm = pl.BlockSpec(memory_space=pltpu.HBM)
    bf16 = jnp.bfloat16
    halves = columns // TILE_COLS
    dma = pltpu.SemaphoreType.DMA
    result = pl.pallas_call(
        functools.partial(sweep, regions, subs),
        out_shape=jax.ShapeDtypeStruct(blocked, jnp.bfloat16),
        in_specs=[hbm] * 7,
        out_specs=vmem,
        scratch_shapes=[
            pltpu.SMEM((OVL_BLK, COLORS), jnp.int32),
            pltpu.SMEM(partner.shape, jnp.int32),
            pltpu.VMEM(blocked, bf16),
            pltpu.VMEM((rows // BLK, BLK, rows), bf16),
            pltpu.VMEM(coupling.shape[2:], bf16),
            pltpu.VMEM(restriction.shape[2:], bf16),
            pltpu.VMEM(coarse_rows.shape[1:], bf16),
            dma((7,)),
            pltpu.VMEM(blocked, jnp.float32),
            pltpu.VMEM(blocked, jnp.float32),
            pltpu.VMEM((rows, columns), jnp.bfloat16),
            pltpu.VMEM((COLORS, pieces) + piece, jnp.bfloat16),
            [pltpu.VMEM((count,) + piece, jnp.bfloat16) for _ in range(COLORS)],
            pltpu.VMEM((COLORS, count) + piece, jnp.bfloat16),
            pltpu.VMEM((COLORS, pieces) + piece, jnp.bfloat16),
            pltpu.VMEM((halves, subs, cp, TILE_COLS), jnp.bfloat16),
            dma((COLORS,)),
            dma((COLORS,)),
            dma((COLORS,)),
            dma((COLORS, halves)),
            dma((halves, subs // 2)),
            dma((halves, subs // 2)),
            dma((halves, subs // 2)),
            dma((halves, subs // 2)),
        ],
        compiler_params=pltpu.CompilerParams(
            collective_id=0, has_side_effects=True, vmem_limit_bytes=56 * 1024 * 1024
        ),
    )(
        right.reshape(blocked),
        local_inverse.reshape(rows // BLK, BLK, rows),
        coupling[0, 0],
        margin_blocks[:, 0, 0, :].T,
        partner,
        restriction[0, 0],
        coarse_rows[0],
    )
    return result.reshape(right_side.shape)


def solution(mesh):
    placed = (
        P("region", "sub", None, None),
        P("region", "sub", None, None),
        P("region", "sub", None, None, None),
        P(None, "region", "sub", None),
        P(),
        P("region", "sub", None, None),
        P("region", "sub", None),
    )
    return jax.shard_map(
        shards,
        mesh=mesh,
        in_specs=placed,
        out_specs=P("region", "sub", None, None),
        check_vma=False,
    )
```
